32 devices in a mesh: slab: 8 (over z, y), face: 4 (over x, core).
Axes of the slice: x: 2, y: 2, z: 4, core: 2. Of those that a mesh axis runs over, the one named last changes fastest.
Arguments:
- rhs: float32 [8, 16, 6, 128], P('slab', 'face'), may hold values from -6 to 6
- iterate: float32 [8, 16, 6, 128], P('slab', 'face'), may hold values from -6 to 6
- op_self: float32 [8, 16, 128, 128], P('slab', 'face'), may hold values from -0.5 to 0.5
- op_couple: float32 [8, 16, 4, 128, 128], P('slab', 'face'), may hold values from -0.25 to 0.25
- fill_slot: int32 [8, 16, 6], P('slab', 'face'), may hold values from 0 to 31
- fill_count: int32 [8, 16], P('slab', 'face'), may hold values from 1 to 6
- fill_blocks: float32 [8, 16, 6, 128, 128], P('slab', 'face'), may hold values from -1.25 to 1.25
- diag_inverse: float32 [8, 16, 128, 128], P('slab', 'face'), may hold values from -1.25 to 1.25
Outputs:
- solution: float32 [8, 16, 6, 128], P('slab', 'face')
- image: float32 [8, 16, 6, 128], P('slab', 'face')
The draws below stay inside these ranges and needn't reach their ends.
All inputs are finite; a program needn't handle non-finite values.
Results may differ from the reference program's by a relative error of at most 0.0003.
Values sent between devices are 32-bit elements; how exact they have to be, the bound alone decides.
A program may use at most 64 MiB of HBM per device.

```python
import jax
import jax.numpy as jnp
from jax import lax

BLK = 128
LOADS = 6
K_FILL = 6
REACH = 2
ROWS_SLAB = 16
SLABS = 8


self_weight = 2.0


chain_gain = 0.94


def slot_table(base_key):
    return jax.random.randint(jax.random.fold_in(base_key, 7), (SLABS, ROWS_SLAB, K_FILL), 0, REACH * ROWS_SLAB, dtype=jnp.int32)


def directions(base_key):
    sign_pattern = jax.random.rademacher(jax.random.fold_in(base_key, 13), (SLABS, ROWS_SLAB, BLK), dtype=jnp.float32)
    return sign_pattern * BLK ** (-0.5)


def draw_fill_slot(key, part):
    return slot_table(key)


def draw_diag_inverse(key, part):
    unit = directions(key)
    noise_key = jax.random.fold_in(key, 17)
    deviation = BLK ** (-0.5)
    extent = (SLABS, ROWS_SLAB, BLK, BLK)
    rough = deviation * jnp.clip(jax.random.normal(noise_key, extent, jnp.float32), -4.0, 4.0)
    coherent = self_weight * unit[:, :, :, None] * unit[:, :, None, :]
    return (rough + coherent).astype(jnp.float32)


def draw_fill_blocks(key, part):
    unit = directions(key)
    slots = slot_table(key)
    nearest = (slots >= (REACH - 1) * ROWS_SLAB).astype(jnp.float32)
    source_row = jnp.clip(slots - (REACH - 1) * ROWS_SLAB, 0, ROWS_SLAB - 1)
    earlier = jnp.concatenate([unit[:1], unit[:-1]], axis=0)
    slab_index = jnp.arange(SLABS, dtype=jnp.int32)[:, None, None]
    read_unit = earlier[slab_index, source_row]
    couple_weight = 2.0 * REACH * chain_gain / ((K_FILL + 1) * self_weight)
    coherent = couple_weight * nearest[:, :, :, None, None] * unit[:, :, None, :, None] * read_unit[:, :, :, None, :]
    noise_key = jax.random.fold_in(key, 19)
    deviation = (BLK * (K_FILL + 1) * 3 // 5) ** (-0.5)
    extent = (SLABS, ROWS_SLAB, K_FILL, BLK, BLK)
    rough = deviation * jnp.clip(jax.random.normal(noise_key, extent, jnp.float32), -4.0, 4.0)
    return (rough + coherent).astype(jnp.float32)


def plant(values, stream_key, low, largest):
    spot = [jax.random.randint(jax.random.fold_in(stream_key, axis), (), 0, length) for axis, length in enumerate(values.shape)]
    main_axis = values.shape.index(max(values.shape))
    beside = spot[:main_axis] + [(spot[main_axis] + 1) % values.shape[main_axis]] + spot[main_axis + 1:]
    return values.at[tuple(spot)].set(low).at[tuple(beside)].set(largest)


def level_of(stream_key, shape, cuts, least, high):
    def one(dim, parts):
        draws = jax.random.uniform(jax.random.fold_in(jax.random.fold_in(stream_key, 6), dim), (parts,), jnp.float32, least / len(cuts), high / len(cuts))
        return jnp.repeat(jnp.exp(draws), shape[dim] // parts).reshape((-1,) + (1,) * (len(shape) - dim - 1))

    level = one(*cuts[0])
    for cut in cuts[1:]:
        level = level * one(*cut)
    return level


def normal_values(own_key, shape, scale, reach, cuts=(), held_as=jnp.bfloat16):
    gain = level_of(own_key, shape, cuts, -0.22, 0.18) if cuts else 1.0
    drawn = jax.random.normal(own_key, shape, jnp.float32) * scale * gain
    return jnp.minimum(jnp.maximum(drawn, -reach), reach).astype(held_as)


def setup_inputs(seed: int = 0) -> dict:
    splits = jax.random.split(jax.random.key(seed), 9)
    rhs = normal_values(splits[0], (SLABS, ROWS_SLAB, LOADS, BLK), 1.0, 6.0, ((0, 8), (1, 4)), jnp.float32)
    iterate = normal_values(splits[1], (SLABS, ROWS_SLAB, LOADS, BLK), 1.0, 6.0, ((0, 8), (1, 4)), jnp.float32)
    op_self = normal_values(splits[2], (SLABS, ROWS_SLAB, BLK, BLK), BLK ** -0.5, 0.5, ((0, 8), (1, 4)), jnp.float32)
    op_couple = normal_values(splits[3], (SLABS, ROWS_SLAB, 4, BLK, BLK), (4 * BLK) ** -0.5, 0.25, ((0, 8), (1, 4)), jnp.float32)
    fill_slot = draw_fill_slot(jax.random.fold_in(splits[8], 71), 0)
    fill_count = plant(jax.random.randint(splits[5], (SLABS, ROWS_SLAB), 1, K_FILL + 1), jax.random.fold_in(splits[5], 1), 1, K_FILL).astype(jnp.int32)
    fill_blocks = draw_fill_blocks(jax.random.fold_in(splits[8], 71), 0)
    diag_inverse = draw_diag_inverse(jax.random.fold_in(splits[8], 71), 0)
    return {"rhs": rhs, "iterate": iterate, "op_self": op_self, "op_couple": op_couple, "fill_slot": fill_slot, "fill_count": fill_count, "fill_blocks": fill_blocks, "diag_inverse": diag_inverse}


def apply_blocks(mats, vecs):
    return jnp.einsum('srij,srlj->srli', mats, vecs, precision=lax.Precision.HIGHEST)


def operator(field, op_self, op_couple):
    padded = jnp.pad(field, ((1, 1), (1, 1), (0, 0), (0, 0)))
    out = apply_blocks(op_self, field)
    out = out + apply_blocks(op_couple[:, :, 0], padded[:-2, 1:-1])
    out = out + apply_blocks(op_couple[:, :, 1], padded[2:, 1:-1])
    out = out + apply_blocks(op_couple[:, :, 2], padded[1:-1, :-2])
    out = out + apply_blocks(op_couple[:, :, 3], padded[1:-1, 2:])
    return out


def reference(rhs, iterate, op_self, op_couple, fill_slot, fill_count, fill_blocks, diag_inverse):
    residual = rhs - operator(iterate, op_self, op_couple)
    rows = residual.shape[1]
    start = jnp.zeros((REACH * rows, LOADS, BLK), jnp.float32)

    def advance(window, inputs):
        res_s, slot_s, count_s, blocks_s, dinv_s = inputs
        picked = window[slot_s]
        used = (jnp.arange(K_FILL, dtype=jnp.int32)[None, :] < count_s[:, None]).astype(jnp.float32)
        acc = jnp.einsum('rkij,rklj->rli', blocks_s, picked * used[:, :, None, None], precision=lax.Precision.HIGHEST)
        solved = jnp.einsum('rij,rlj->rli', dinv_s, res_s - acc, precision=lax.Precision.HIGHEST)
        window = jnp.concatenate([window[rows:], solved], axis=0)
        return window, solved

    _, solution = lax.scan(advance, start, (residual, fill_slot, fill_count, fill_blocks, diag_inverse))
    image = operator(solution, op_self, op_couple)
    return solution, image
```

```python
import functools

import jax
import jax.numpy as jnp
from jax import lax
from jax.experimental import pallas as pl
from jax.experimental.pallas import tpu as pltpu
from jax.sharding import PartitionSpec as P

MESH = pl.DeviceIdType.MESH
NT = (((1,), (1,)), ((), ()))
F32, BF16 = jnp.float32, jnp.bfloat16


def halves(x):
    high = x.astype(BF16)
    return high, (x - high.astype(F32)).astype(BF16)


def rows_of(v):
    high = v.astype(BF16).astype(F32)
    return jnp.concatenate([high, v - high], axis=0).astype(BF16)


def product(x, w):
    y = lax.dot_general(x, w, NT, preferred_element_type=F32)
    n = w.shape[0] // 2
    return y[:8, :n] + (y[:8, n:] + y[8:, :n])


def kernel(
    dims,
    rhs, it, ops, opc, slot, cnt, fill, dinv,
    sol_out, img_out,
    v_rhs, v_it, v_ops, v_opc, v_fill, v_dinv,
    it_prev, it_next, it_lo, it_hi,
    w_op, w_fill, w_inv,
    part, sol, v_sol, v_img, win1, win2, s_next, s_lo, s_hi,
    load_sem, out_sem, it_send, it_recv, one_send, one_recv, two_send, two_recv, near_send, near_recv,
):
    slabs, faces, rows, loads, blk, fills = dims
    s, f = lax.axis_index("slab"), lax.axis_index("face")
    own = rows * loads
    slab_rows = faces * rows
    has_prev, has_next = s > 0, s < slabs - 1
    has_lo, has_hi = f > 0, f < faces - 1

    pairs = ((it, v_it), (rhs, v_rhs), (ops, v_ops), (opc, v_opc), (dinv, v_dinv), (fill, v_fill))
    loading = [
        pltpu.make_async_copy(a.at[0], b, load_sem.at[n]) for n, (a, b) in enumerate(pairs)
    ]
    for c in loading:
        c.start()

    barrier = pltpu.get_barrier_semaphore()

    def greet(ok, who):
        @pl.when(ok)
        def _():
            pl.semaphore_signal(barrier, inc=1, device_id=who, device_id_type=MESH)

    greet(has_next, (s + 1, f))
    greet(has_lo, (s, f - 1))
    greet(has_hi, (s, f + 1))
    for g in range(faces):
        greet(has_prev, (s - 1, g))
    for g in range(faces):
        greet(s > 1, (s - 2, g))

    peers = has_prev.astype(jnp.int32) + has_lo.astype(jnp.int32) + has_hi.astype(jnp.int32)
    peers = peers + faces * (has_next.astype(jnp.int32) + (s < slabs - 2).astype(jnp.int32))
    pl.semaphore_wait(barrier, peers)

    def remote(src, dst, a, b, who):
        return pltpu.make_async_remote_copy(
            src_ref=src, dst_ref=dst, send_sem=a, recv_sem=b, device_id=who, device_id_type=MESH
        )

    halo = (
        (has_next, has_prev, it.at[0], it_prev, (s + 1, f)),
        (has_prev, has_next, it.at[0], it_next, (s - 1, f)),
        (has_hi, has_lo, it.at[0, pl.ds(rows - 1, 1)], it_lo, (s, f + 1)),
        (has_lo, has_hi, it.at[0, pl.ds(0, 1)], it_hi, (s, f - 1)),
    )
    halo_copies = []
    for n, (sends, gets, src, dst, who) in enumerate(halo):
        c = remote(src, dst, it_send.at[n], it_recv.at[n], who)
        halo_copies.append(c)
        pl.when(sends)(c.start)

        @pl.when(jnp.logical_not(gets))
        def _(dst=dst):
            dst[...] = jnp.zeros_like(dst)

    @pl.when(jnp.logical_not(has_prev))
    def _():
        win1[...] = jnp.zeros_like(win1)

    @pl.when(jnp.logical_not(has_next))
    def _():
        s_next[...] = jnp.zeros_like(s_next)

    @pl.when(jnp.logical_not(has_lo))
    def _():
        s_lo[...] = jnp.zeros_like(s_lo)

    @pl.when(jnp.logical_not(has_hi))
    def _():
        s_hi[...] = jnp.zeros_like(s_hi)

    for c in loading[:4]:
        c.wait()

    for r in range(rows):
        blocks = (v_ops[r], v_opc[r, 0], v_opc[r, 2], v_opc[r, 3], v_opc[r, 1])
        for n, m in enumerate(blocks):
            high, low = halves(m)
            w_op[r, :blk, n * blk : (n + 1) * blk] = high
            w_op[r, blk:, n * blk : (n + 1) * blk] = low
    loading[4].wait()
    for r in range(rows):
        high, low = halves(v_dinv[r])
        w_inv[r, :blk] = high
        w_inv[r, blk:] = low

    for c, (sends, gets, *_) in zip(halo_copies, halo):
        pl.when(gets)(c.wait_recv)

    fill_up = jnp.zeros((8 - loads, blk), F32)

    def up(v):
        return jnp.concatenate([v, fill_up], axis=0)

    for r in range(rows):
        before = it_lo[0] if r == 0 else v_it[r - 1]
        after = it_hi[0] if r == rows - 1 else v_it[r + 1]
        x = jnp.concatenate(
            [rows_of(up(v)) for v in (v_it[r], it_prev[r], before, after, it_next[r])], axis=1
        )
        residual = up(v_rhs[r]) - product(x, w_op[r])
        part[r] = product(rows_of(residual), w_inv[r])

    def to_next(g):
        return remote(
            sol, win1.at[pl.ds(f * own, own)], one_send.at[g], one_recv.at[f], (s + 1, g)
        )

    def to_second(g):
        return remote(
            sol, win2.at[pl.ds(f * own, own)], two_send.at[g], two_recv.at[f], (s + 2, g)
        )

    def arrive(win, sem, g):
        return remote(sol, win.at[pl.ds(g * own, own)], one_send.at[g], sem.at[g], (s, f))

    near = (
        (has_prev, has_next, sol, s_next, (s - 1, f)),
        (has_hi, has_lo, sol.at[pl.ds(own - 8, 8)], s_lo, (s, f + 1)),
        (has_lo, has_hi, sol.at[pl.ds(0, 8)], s_hi, (s, f - 1)),
    )
    near_copies = [
        remote(src, dst, near_send.at[n], near_recv.at[n], who)
        for n, (_, _, src, dst, who) in enumerate(near)
    ]

    def spread():
        @pl.when(has_next)
        def _():
            for g in range(faces):
                to_next(g).start()

        for c, (sends, *_) in zip(near_copies[1:], near[1:]):
            pl.when(sends)(c.start)
        pl.when(has_prev)(near_copies[0].start)

        @pl.when(s < slabs - 2)
        def _():
            for g in range(faces):
                to_second(g).start()

    @pl.when(jnp.logical_not(has_prev))
    def _():
        for r in range(rows):
            sol[r * loads : (r + 1) * loads] = part[r][:loads]
        spread()

    loading[5].wait()

    @pl.when(has_prev)
    def _():
        for r in range(rows):
            left = jnp.concatenate([w_inv[r, :blk], w_inv[r, blk:]], axis=1)
            for k in range(fills):
                high, low = halves(v_fill[r, k])
                right = jnp.concatenate(
                    [
                        jnp.concatenate([high, low], axis=1),
                        jnp.concatenate([high, jnp.zeros_like(low)], axis=1),
                    ],
                    axis=0,
                )
                y = jnp.dot(left, right, preferred_element_type=F32)
                high, low = halves(y[:, :blk] + y[:, blk:])
                w_fill[r, :blk, k * blk : (k + 1) * blk] = high
                w_fill[r, blk:, k * blk : (k + 1) * blk] = low

    def gathered(win, r, base):
        xs = []
        for k in range(fills):
            q = slot[0, r, k] - base
            ok = jnp.logical_and(jnp.logical_and(q >= 0, q < slab_rows), k < cnt[0, r])
            q = jnp.clip(q, 0, slab_rows - 1)
            v = win[pl.ds(q * loads, 8), :]
            xs.append(rows_of(jnp.where(ok, v, 0.0)))
        return jnp.concatenate(xs, axis=1)

    @pl.when(s > 1)
    def _():
        for g in range(faces):
            arrive(win2, two_recv, g).wait_recv()
        for r in range(rows):
            part[r] = part[r] - product(gathered(win2, r, 0), w_fill[r])

    @pl.when(has_prev)
    def _():
        for g in range(faces):
            arrive(win1, one_recv, g).wait_recv()
        for r in range(rows):
            y = part[r] - product(gathered(win1, r, slab_rows), w_fill[r])
            sol[r * loads : (r + 1) * loads] = y[:loads]
        spread()

    for r in range(rows):
        v_sol[r] = sol[r * loads : (r + 1) * loads]
    sol_copy = pltpu.make_async_copy(v_sol, sol_out.at[0], out_sem.at[0])
    sol_copy.start()

    def mine(ref, r):
        return rows_of(up(ref[r * loads : (r + 1) * loads]))

    for r in range(rows):
        x = jnp.concatenate(
            [
                mine(sol, r),
                rows_of(up(win1[pl.ds(f * own + r * loads, loads), :])),
            ],
            axis=1,
        )
        part[r] = product(x, w_op[r, :, : 2 * blk])
    for c, (_, gets, *_) in zip(near_copies[1:], near[1:]):
        pl.when(gets)(c.wait_recv)
    for r in range(rows):
        before = rows_of(up(s_lo[8 - loads :])) if r == 0 else mine(sol, r - 1)
        after = rows_of(up(s_hi[:loads])) if r == rows - 1 else mine(sol, r + 1)
        x = jnp.concatenate([before, after], axis=1)
        part[r] = part[r] + product(x, w_op[r, :, 2 * blk : 4 * blk])
    pl.when(has_next)(near_copies[0].wait_recv)
    for r in range(rows):
        y = part[r] + product(mine(s_next, r), w_op[r, :, 4 * blk :])
        v_img[r] = y[:loads]
    img_copy = pltpu.make_async_copy(v_img, img_out.at[0], out_sem.at[1])
    img_copy.start()

    for c, (sends, *_) in zip(halo_copies, halo):
        pl.when(sends)(c.wait_send)
    for c, (sends, *_) in zip(near_copies, near):
        pl.when(sends)(c.wait_send)

    @pl.when(has_next)
    def _():
        for g in range(faces):
            to_next(g).wait_send()

    @pl.when(s < slabs - 2)
    def _():
        for g in range(faces):
            to_second(g).wait_send()

    sol_copy.wait()
    img_copy.wait()


def body(slabs, faces, *args):
    rhs, _, ops, opc, _, _, fill, dinv = args
    _, rows, loads, blk = rhs.shape
    fills = fill.shape[2]
    own = rows * loads
    dims = (slabs, faces, rows, loads, blk, fills)
    small = (rows, loads, blk)
    anywhere = pl.BlockSpec(memory_space=pl.ANY)
    smem = pl.BlockSpec(memory_space=pltpu.SMEM)
    out = jax.ShapeDtypeStruct(rhs.shape, F32)
    dma = pltpu.SemaphoreType.DMA
    return pl.pallas_call(
        functools.partial(kernel, dims),
        out_shape=(out, out),
        in_specs=[anywhere] * 4 + [smem] * 2 + [anywhere] * 2,
        out_specs=(anywhere, anywhere),
        scratch_shapes=[
            pltpu.VMEM(small, F32),
            pltpu.VMEM(small, F32),
            pltpu.VMEM(ops.shape[1:], F32),
            pltpu.VMEM(opc.shape[1:], F32),
            pltpu.VMEM(fill.shape[1:], F32),
            pltpu.VMEM(dinv.shape[1:], F32),
            pltpu.VMEM(small, F32),
            pltpu.VMEM(small, F32),
            pltpu.VMEM((1, loads, blk), F32),
            pltpu.VMEM((1, loads, blk), F32),
            pltpu.VMEM((rows, 2 * blk, 5 * blk), BF16),
            pltpu.VMEM((rows, 2 * blk, fills * blk), BF16),
            pltpu.VMEM((rows, 2 * blk, blk), BF16),
            pltpu.VMEM((rows, 8, blk), F32),
            pltpu.VMEM((own, blk), F32),
            pltpu.VMEM(small, F32),
            pltpu.VMEM(small, F32),
            pltpu.VMEM((faces * own + 8, blk), F32),
            pltpu.VMEM((faces * own + 8, blk), F32),
            pltpu.VMEM((own, blk), F32),
            pltpu.VMEM((8, blk), F32),
            pltpu.VMEM((8, blk), F32),
            dma((6,)),
            dma((2,)),
            dma((4,)),
            dma((4,)),
            dma((faces,)),
            dma((faces,)),
            dma((faces,)),
            dma((faces,)),
            dma((3,)),
            dma((3,)),
        ],
        compiler_params=pltpu.CompilerParams(
            collective_id=0, has_side_effects=True, vmem_limit_bytes=32 * 2**20
        ),
        cost_estimate=pl.CostEstimate(
            flops=2 * rows * (2 * 5 + fills + 1) * blk * blk * loads,
            bytes_accessed=4 * rows * (6 + fills) * blk * blk,
            transcendentals=0,
        ),
    )(*args)


def solution(mesh):
    four = P("slab", "face", None, None)
    five = P("slab", "face", None, None, None)
    return jax.shard_map(
        functools.partial(body, mesh.shape["slab"], mesh.shape["face"]),
        mesh=mesh,
        in_specs=(four, four, four, five, P("slab", "face", None), P("slab", "face"), five, four),
        out_specs=(four, four),
        check_vma=False,
    )
```

```python
import functools

import jax
import jax.numpy as jnp
from jax import lax
from jax.experimental import pallas as pl
from jax.experimental.pallas import tpu as pltpu
from jax.sharding import PartitionSpec as P

MESH = pl.DeviceIdType.MESH
F32, BF16 = jnp.float32, jnp.bfloat16


def halves(x):
    high = x.astype(BF16)
    return high, (x - high.astype(F32)).astype(BF16)


def rows_of(v):
    high = v.astype(BF16).astype(F32)
    return jnp.concatenate([high, v - high], axis=0).astype(BF16)


def product(x, w):
    y = jnp.dot(x, w, preferred_element_type=F32)
    n = w.shape[1] // 2
    return y[:8, :n] + (y[:8, n:] + y[8:, :n])


def kernel(
    dims,
    rhs, it, ops, opc, slot_in, cnt_in, fill, dinv,
    sol_out, img_out,
    slot, cnt, v_rhs, v_it, v_ops, v_opc, v_fill, v_dinv,
    it_prev, it_next, it_lo, it_hi,
    w_op, w_fill, w_inv,
    part, sol, v_sol, v_img, win1, win2, s_next, s_lo, s_hi,
    load_sem, out_sem, it_send, it_recv, one_send, one_recv, two_send, two_recv, near_send, near_recv,
):
    slabs, faces, rows, loads, blk, fills = dims
    s, f = lax.axis_index("slab"), lax.axis_index("face")
    own = rows * loads
    slab_rows = faces * rows
    has_prev, has_next = s > 0, s < slabs - 1
    has_lo, has_hi = f > 0, f < faces - 1

    pairs = (
        (it.at[0], v_it), (rhs.at[0], v_rhs), (ops.at[0], v_ops), (opc.at[0], v_opc),
        (dinv.at[0], v_dinv), (fill.at[0], v_fill), (slot_in, slot), (cnt_in, cnt),
    )
    loading = [
        pltpu.make_async_copy(a, b, load_sem.at[n]) for n, (a, b) in enumerate(pairs)
    ]
    for c in loading:
        c.start()

    barrier = pltpu.get_barrier_semaphore()

    def greet(ok, who):
        @pl.when(ok)
        def _():
            pl.semaphore_signal(barrier, inc=1, device_id=who, device_id_type=MESH)

    greet(has_next, (s + 1, f))
    greet(has_lo, (s, f - 1))
    greet(has_hi, (s, f + 1))
    for g in range(faces):
        greet(has_prev, (s - 1, g))
    for g in range(faces):
        greet(s > 1, (s - 2, g))

    peers = has_prev.astype(jnp.int32) + has_lo.astype(jnp.int32) + has_hi.astype(jnp.int32)
    peers = peers + faces * (has_next.astype(jnp.int32) + (s < slabs - 2).astype(jnp.int32))
    pl.semaphore_wait(barrier, peers)

    def remote(src, dst, a, b, who):
        return pltpu.make_async_remote_copy(
            src_ref=src, dst_ref=dst, send_sem=a, recv_sem=b, device_id=who, device_id_type=MESH
        )

    halo = (
        (has_next, has_prev, it.at[0], it_prev, (s + 1, f)),
        (has_prev, has_next, it.at[0], it_next, (s - 1, f)),
        (has_hi, has_lo, it.at[0], it_lo, (s, f + 1)),
        (has_lo, has_hi, it.at[0], it_hi, (s, f - 1)),
    )
    halo_copies = []
    for n, (sends, gets, src, dst, who) in enumerate(halo):
        c = remote(src, dst, it_send.at[n], it_recv.at[n], who)
        halo_copies.append(c)
        pl.when(sends)(c.start)

        @pl.when(jnp.logical_not(gets))
        def _(dst=dst):
            dst[...] = jnp.zeros_like(dst)

    @pl.when(jnp.logical_not(has_prev))
    def _():
        win1[...] = jnp.zeros_like(win1)

    @pl.when(jnp.logical_not(has_next))
    def _():
        s_next[...] = jnp.zeros_like(s_next)

    @pl.when(jnp.logical_not(has_lo))
    def _():
        s_lo[...] = jnp.zeros_like(s_lo)

    @pl.when(jnp.logical_not(has_hi))
    def _():
        s_hi[...] = jnp.zeros_like(s_hi)

    for c in loading[:4]:
        c.wait()

    for r in range(rows):
        blocks = (v_ops[r], v_opc[r, 0], v_opc[r, 2], v_opc[r, 3], v_opc[r, 1])
        for n, m in enumerate(blocks):
            high, low = halves(m.T)
            w_op[r, n * blk : (n + 1) * blk, :blk] = high
            w_op[r, n * blk : (n + 1) * blk, blk:] = low
    loading[4].wait()
    for r in range(rows):
        high, low = halves(v_dinv[r].T)
        w_inv[r, :, :blk] = high
        w_inv[r, :, blk:] = low

    for c, (sends, gets, *_) in zip(halo_copies, halo):
        pl.when(gets)(c.wait_recv)

    fill_up = jnp.zeros((8 - loads, blk), F32)

    def up(v):
        return jnp.concatenate([v, fill_up], axis=0)

    for r in range(rows):
        before = it_lo[:, rows - 1] if r == 0 else v_it[:, r - 1]
        after = it_hi[:, 0] if r == rows - 1 else v_it[:, r + 1]
        x = jnp.concatenate(
            [rows_of(up(v)) for v in (v_it[:, r], it_prev[:, r], before, after, it_next[:, r])], axis=1
        )
        residual = up(v_rhs[:, r]) - product(x, w_op[r])
        part[r] = product(rows_of(residual), w_inv[r])

    def to_next(g):
        return remote(
            sol, win1.at[pl.ds(f * own, own)], one_send.at[g], one_recv.at[f], (s + 1, g)
        )

    def to_second(g):
        return remote(
            sol, win2.at[pl.ds(f * own, own)], two_send.at[g], two_recv.at[f], (s + 2, g)
        )

    def arrive(win, sem, g):
        return remote(sol, win.at[pl.ds(g * own, own)], one_send.at[g], sem.at[g], (s, f))

    near = (
        (has_prev, has_next, sol, s_next, (s - 1, f)),
        (has_hi, has_lo, sol.at[pl.ds(own - 8, 8)], s_lo, (s, f + 1)),
        (has_lo, has_hi, sol.at[pl.ds(0, 8)], s_hi, (s, f - 1)),
    )
    near_copies = [
        remote(src, dst, near_send.at[n], near_recv.at[n], who)
        for n, (_, _, src, dst, who) in enumerate(near)
    ]

    def spread():
        @pl.when(has_next)
        def _():
            for g in range(faces):
                to_next(g).start()

        for c, (sends, *_) in zip(near_copies[1:], near[1:]):
            pl.when(sends)(c.start)
        pl.when(has_prev)(near_copies[0].start)

        @pl.when(s < slabs - 2)
        def _():
            for g in range(faces):
                to_second(g).start()

    @pl.when(jnp.logical_not(has_prev))
    def _():
        for r in range(rows):
            sol[r * loads : (r + 1) * loads] = part[r][:loads]
        spread()

    for c in loading[5:]:
        c.wait()

    @pl.when(has_prev)
    def _():
        for r in range(rows):
            left = jnp.concatenate(halves(v_dinv[r]), axis=1)
            for k in range(fills):
                high, low = halves(v_fill[r, k])
                right = jnp.concatenate(
                    [
                        jnp.concatenate([high, low], axis=1),
                        jnp.concatenate([high, jnp.zeros_like(low)], axis=1),
                    ],
                    axis=0,
                )
                y = jnp.dot(left, right, preferred_element_type=F32)
                high, low = halves((y[:, :blk] + y[:, blk:]).T)
                w_fill[r, k * blk : (k + 1) * blk, :blk] = high
                w_fill[r, k * blk : (k + 1) * blk, blk:] = low

    def gathered(win, r, base):
        xs = []
        for k in range(fills):
            q = slot[0, r, k] - base
            ok = jnp.logical_and(jnp.logical_and(q >= 0, q < slab_rows), k < cnt[0, r])
            q = jnp.clip(q, 0, slab_rows - 1)
            v = win[pl.ds(q * loads, 8), :]
            xs.append(rows_of(jnp.where(ok, v, 0.0)))
        return jnp.concatenate(xs, axis=1)

    @pl.when(s > 1)
    def _():
        for g in range(faces):
            arrive(win2, two_recv, g).wait_recv()
        for r in range(rows):
            part[r] = part[r] - product(gathered(win2, r, 0), w_fill[r])

    @pl.when(has_prev)
    def _():
        for g in range(faces):
            arrive(win1, one_recv, g).wait_recv()
        for r in range(rows):
            y = part[r] - product(gathered(win1, r, slab_rows), w_fill[r])
            sol[r * loads : (r + 1) * loads] = y[:loads]
        spread()

    for r in range(rows):
        v_sol[:, r] = sol[r * loads : (r + 1) * loads]
    sol_copy = pltpu.make_async_copy(v_sol, sol_out.at[0], out_sem.at[0])
    sol_copy.start()

    def mine(ref, r):
        return rows_of(up(ref[r * loads : (r + 1) * loads]))

    for r in range(rows):
        x = jnp.concatenate(
            [
                mine(sol, r),
                rows_of(up(win1[pl.ds(f * own + r * loads, loads), :])),
            ],
            axis=1,
        )
        part[r] = product(x, w_op[r, : 2 * blk])
    for c, (_, gets, *_) in zip(near_copies[1:], near[1:]):
        pl.when(gets)(c.wait_recv)
    for r in range(rows):
        before = rows_of(up(s_lo[8 - loads :])) if r == 0 else mine(sol, r - 1)
        after = rows_of(up(s_hi[:loads])) if r == rows - 1 else mine(sol, r + 1)
        x = jnp.concatenate([before, after], axis=1)
        part[r] = part[r] + product(x, w_op[r, 2 * blk : 4 * blk])
    pl.when(has_next)(near_copies[0].wait_recv)
    for r in range(rows):
        y = part[r] + product(mine(s_next, r), w_op[r, 4 * blk :])
        v_img[:, r] = y[:loads]
    img_copy = pltpu.make_async_copy(v_img, img_out.at[0], out_sem.at[1])
    img_copy.start()

    for c, (sends, *_) in zip(halo_copies, halo):
        pl.when(sends)(c.wait_send)
    for c, (sends, *_) in zip(near_copies, near):
        pl.when(sends)(c.wait_send)

    @pl.when(has_next)
    def _():
        for g in range(faces):
            to_next(g).wait_send()

    @pl.when(s < slabs - 2)
    def _():
        for g in range(faces):
            to_second(g).wait_send()

    sol_copy.wait()
    img_copy.wait()


def body(slabs, faces, *args):
    rhs, it, ops, opc, slot, cnt, fill, dinv = args
    _, rows, loads, blk = rhs.shape
    fills = fill.shape[2]
    own = rows * loads
    dims = (slabs, faces, rows, loads, blk, fills)
    small = (loads, rows, blk)
    anywhere = pl.BlockSpec(memory_space=pl.ANY)
    out = jax.ShapeDtypeStruct((1,) + small, F32)
    dma = pltpu.SemaphoreType.DMA
    outs = pl.pallas_call(
        functools.partial(kernel, dims),
        out_shape=(out, out),
        in_specs=[anywhere] * 8,
        out_specs=(anywhere, anywhere),
        scratch_shapes=[
            pltpu.SMEM(slot.shape, jnp.int32),
            pltpu.SMEM(cnt.shape, jnp.int32),
            pltpu.VMEM(small, F32),
            pltpu.VMEM(small, F32),
            pltpu.VMEM(ops.shape[1:], F32),
            pltpu.VMEM(opc.shape[1:], F32),
            pltpu.VMEM(fill.shape[1:], F32),
            pltpu.VMEM(dinv.shape[1:], F32),
            pltpu.VMEM(small, F32),
            pltpu.VMEM(small, F32),
            pltpu.VMEM(small, F32),
            pltpu.VMEM(small, F32),
            pltpu.VMEM((rows, 5 * blk, 2 * blk), BF16),
            pltpu.VMEM((rows, fills * blk, 2 * blk), BF16),
            pltpu.VMEM((rows, blk, 2 * blk), BF16),
            pltpu.VMEM((rows, 8, blk), F32),
            pltpu.VMEM((own, blk), F32),
            pltpu.VMEM(small, F32),
            pltpu.VMEM(small, F32),
            pltpu.VMEM((faces * own + 8, blk), F32),
            pltpu.VMEM((faces * own + 8, blk), F32),
            pltpu.VMEM((own, blk), F32),
            pltpu.VMEM((8, blk), F32),
            pltpu.VMEM((8, blk), F32),
            dma((8,)),
            dma((2,)),
            dma((4,)),
            dma((4,)),
            dma((faces,)),
            dma((faces,)),
            dma((faces,)),
            dma((faces,)),
            dma((3,)),
            dma((3,)),
        ],
        compiler_params=pltpu.CompilerParams(
            collective_id=0, has_side_effects=True, vmem_limit_bytes=60 * 2**20
        ),
        cost_estimate=pl.CostEstimate(
            flops=2 * rows * (2 * 5 + fills + 1) * blk * blk * loads,
            bytes_accessed=4 * rows * (6 + fills) * blk * blk,
            transcendentals=0,
        ),
    )(jnp.swapaxes(rhs, 1, 2), jnp.swapaxes(it, 1, 2), ops, opc, slot, cnt, fill, dinv)
    return tuple(jnp.swapaxes(o, 1, 2) for o in outs)


def solution(mesh):
    four = P("slab", "face", None, None)
    five = P("slab", "face", None, None, None)
    return jax.shard_map(
        functools.partial(body, mesh.shape["slab"], mesh.shape["face"]),
        mesh=mesh,
        in_specs=(four, four, four, five, P("slab", "face", None), P("slab", "face"), five, four),
        out_specs=(four, four),
        check_vma=False,
    )
```

```python
import functools

import jax
import jax.numpy as jnp
from jax import lax
from jax.experimental import pallas as pl
from jax.experimental.pallas import tpu as pltpu
from jax.sharding import PartitionSpec as P

MESH = pl.DeviceIdType.MESH
F32, BF16 = jnp.float32, jnp.bfloat16


def halves(x):
    high = x.astype(BF16)
    return high, (x - high.astype(F32)).astype(BF16)


def rows_of(v):
    high = v.astype(BF16).astype(F32)
    return jnp.concatenate([high, v - high], axis=0).astype(BF16)


def product(x, w):
    y = jnp.dot(x, w, preferred_element_type=F32)
    n = w.shape[1] // 2
    return y[:8, :n] + (y[:8, n:] + y[8:, :n])


def kernel(
    dims,
    rhs, it, ops, opc, slot_in, cnt_in, fill, dinv,
    out,
    slot, cnt, v_rhs, v_it, v_ops, v_opc, v_fill, v_dinv,
    it_prev, it_next, it_lo, it_hi,
    w_op, w_fill, w_inv,
    part, sol, win1, win2, s_next, s_lo, s_hi,
    load_sem, it_send, it_recv, one_send, one_recv, two_send, two_recv, near_send, near_recv,
):
    slabs, faces, rows, loads, blk, fills = dims
    s, f = lax.axis_index("slab"), lax.axis_index("face")
    own = rows * loads
    slab_rows = faces * rows
    has_prev, has_next = s > 0, s < slabs - 1
    has_lo, has_hi = f > 0, f < faces - 1

    pairs = (
        (it.at[0], v_it), (rhs.at[0], v_rhs), (ops.at[0], v_ops), (opc.at[0], v_opc),
        (dinv.at[0], v_dinv), (fill.at[0], v_fill), (slot_in, slot), (cnt_in, cnt),
    )
    loading = [
        pltpu.make_async_copy(a, b, load_sem.at[n]) for n, (a, b) in enumerate(pairs)
    ]
    for c in loading:
        c.start()

    barrier = pltpu.get_barrier_semaphore()

    def greet(ok, who):
        @pl.when(ok)
        def _():
            pl.semaphore_signal(barrier, inc=1, device_id=who, device_id_type=MESH)

    greet(has_next, (s + 1, f))
    greet(has_lo, (s, f - 1))
    greet(has_hi, (s, f + 1))
    for g in range(faces):
        greet(has_prev, (s - 1, g))
    for g in range(faces):
        greet(s > 1, (s - 2, g))

    for c in loading[:4]:
        c.wait()

    for r in range(rows):
        blocks = (v_ops[r], v_opc[r, 0], v_opc[r, 2], v_opc[r, 3], v_opc[r, 1])
        for n, m in enumerate(blocks):
            high, low = halves(m.T)
            w_op[r, n * blk : (n + 1) * blk, :blk] = high
            w_op[r, n * blk : (n + 1) * blk, blk:] = low
    peers = has_prev.astype(jnp.int32) + has_lo.astype(jnp.int32) + has_hi.astype(jnp.int32)
    peers = peers + faces * (has_next.astype(jnp.int32) + (s < slabs - 2).astype(jnp.int32))
    pl.semaphore_wait(barrier, peers)

    def remote(src, dst, a, b, who):
        return pltpu.make_async_remote_copy(
            src_ref=src, dst_ref=dst, send_sem=a, recv_sem=b, device_id=who, device_id_type=MESH
        )

    halo = (
        (has_next, has_prev, it.at[0], it_prev, (s + 1, f)),
        (has_prev, has_next, it.at[0], it_next, (s - 1, f)),
        (has_hi, has_lo, it.at[0], it_lo, (s, f + 1)),
        (has_lo, has_hi, it.at[0], it_hi, (s, f - 1)),
    )
    halo_copies = []
    for n, (sends, gets, src, dst, who) in enumerate(halo):
        c = remote(src, dst, it_send.at[n], it_recv.at[n], who)
        halo_copies.append(c)
        pl.when(sends)(c.start)

        @pl.when(jnp.logical_not(gets))
        def _(dst=dst):
            dst[...] = jnp.zeros_like(dst)

    @pl.when(jnp.logical_not(has_prev))
    def _():
        win1[...] = jnp.zeros_like(win1)

    @pl.when(jnp.logical_not(has_next))
    def _():
        s_next[...] = jnp.zeros_like(s_next)

    @pl.when(jnp.logical_not(has_lo))
    def _():
        s_lo[...] = jnp.zeros_like(s_lo)

    @pl.when(jnp.logical_not(has_hi))
    def _():
        s_hi[...] = jnp.zeros_like(s_hi)

    loading[4].wait()
    for r in range(rows):
        high, low = halves(v_dinv[r].T)
        w_inv[r, :, :blk] = high
        w_inv[r, :, blk:] = low

    for c, (sends, gets, *_) in zip(halo_copies, halo):
        pl.when(gets)(c.wait_recv)

    fill_up = jnp.zeros((8 - loads, blk), F32)

    def up(v):
        return jnp.concatenate([v, fill_up], axis=0)

    for r in range(rows):
        before = it_lo[:, rows - 1] if r == 0 else v_it[:, r - 1]
        after = it_hi[:, 0] if r == rows - 1 else v_it[:, r + 1]
        x = jnp.concatenate(
            [rows_of(up(v)) for v in (v_it[:, r], it_prev[:, r], before, after, it_next[:, r])], axis=1
        )
        residual = up(v_rhs[:, r]) - product(x, w_op[r])
        part[r] = product(rows_of(residual), w_inv[r])

    def to_next(g):
        return remote(
            sol, win1.at[pl.ds(f * own, own)], one_send.at[g], one_recv.at[f], (s + 1, g)
        )

    def to_second(g):
        return remote(
            sol, win2.at[pl.ds(f * own, own)], two_send.at[g], two_recv.at[f], (s + 2, g)
        )

    def arrive(win, sem, g):
        return remote(sol, win.at[pl.ds(g * own, own)], one_send.at[g], sem.at[g], (s, f))

    near = (
        (has_prev, has_next, sol, s_next, (s - 1, f)),
        (has_hi, has_lo, sol.at[pl.ds(own - 8, 8)], s_lo, (s, f + 1)),
        (has_lo, has_hi, sol.at[pl.ds(0, 8)], s_hi, (s, f - 1)),
    )
    near_copies = [
        remote(src, dst, near_send.at[n], near_recv.at[n], who)
        for n, (_, _, src, dst, who) in enumerate(near)
    ]

    def spread():
        @pl.when(has_next)
        def _():
            for g in range(faces):
                to_next(g).start()

        for c, (sends, *_) in zip(near_copies[1:], near[1:]):
            pl.when(sends)(c.start)
        pl.when(has_prev)(near_copies[0].start)

        @pl.when(s < slabs - 2)
        def _():
            for g in range(faces):
                to_second(g).start()

    @pl.when(jnp.logical_not(has_prev))
    def _():
        for r in range(rows):
            sol[r * loads : (r + 1) * loads] = part[r][:loads]
        spread()

    for c in loading[5:]:
        c.wait()

    @pl.when(has_prev)
    def _():
        for r in range(rows):
            left = jnp.concatenate(halves(v_dinv[r]), axis=1)
            for k in range(fills):
                high, low = halves(v_fill[r, k])
                right = jnp.concatenate(
                    [
                        jnp.concatenate([high, low], axis=1),
                        jnp.concatenate([high, jnp.zeros_like(low)], axis=1),
                    ],
                    axis=0,
                )
                y = jnp.dot(left, right, preferred_element_type=F32)
                high, low = halves((y[:, :blk] + y[:, blk:]).T)
                w_fill[r, k * blk : (k + 1) * blk, :blk] = high
                w_fill[r, k * blk : (k + 1) * blk, blk:] = low

    def gathered(win, r, base):
        xs = []
        for k in range(fills):
            q = slot[0, r, k] - base
            ok = jnp.logical_and(jnp.logical_and(q >= 0, q < slab_rows), k < cnt[0, r])
            q = jnp.clip(q, 0, slab_rows - 1)
            v = win[pl.ds(q * loads, 8), :]
            xs.append(rows_of(jnp.where(ok, v, 0.0)))
        return jnp.concatenate(xs, axis=1)

    @pl.when(s > 1)
    def _():
        for g in range(faces):
            arrive(win2, two_recv, g).wait_recv()
        for r in range(rows):
            part[r] = part[r] - product(gathered(win2, r, 0), w_fill[r])

    @pl.when(has_prev)
    def _():
        for g in range(faces):
            arrive(win1, one_recv, g).wait_recv()
        for r in range(rows):
            y = part[r] - product(gathered(win1, r, slab_rows), w_fill[r])
            sol[r * loads : (r + 1) * loads] = y[:loads]
        spread()

    for r in range(rows):
        out[0, :, r] = sol[r * loads : (r + 1) * loads]

    def mine(ref, r):
        return rows_of(up(ref[r * loads : (r + 1) * loads]))

    for r in range(rows):
        x = jnp.concatenate(
            [
                mine(sol, r),
                rows_of(up(win1[pl.ds(f * own + r * loads, loads), :])),
            ],
            axis=1,
        )
        part[r] = product(x, w_op[r, : 2 * blk])
    for c, (_, gets, *_) in zip(near_copies[1:], near[1:]):
        pl.when(gets)(c.wait_recv)
    for r in range(rows):
        before = rows_of(up(s_lo[8 - loads :])) if r == 0 else mine(sol, r - 1)
        after = rows_of(up(s_hi[:loads])) if r == rows - 1 else mine(sol, r + 1)
        x = jnp.concatenate([before, after], axis=1)
        part[r] = part[r] + product(x, w_op[r, 2 * blk : 4 * blk])
    pl.when(has_next)(near_copies[0].wait_recv)
    for r in range(rows):
        y = part[r] + product(mine(s_next, r), w_op[r, 4 * blk :])
        out[1, :, r] = y[:loads]

    for c, (sends, *_) in zip(halo_copies, halo):
        pl.when(sends)(c.wait_send)
    for c, (sends, *_) in zip(near_copies, near):
        pl.when(sends)(c.wait_send)

    @pl.when(has_next)
    def _():
        for g in range(faces):
            to_next(g).wait_send()

    @pl.when(s < slabs - 2)
    def _():
        for g in range(faces):
            to_second(g).wait_send()


def body(slabs, faces, *args):
    rhs, it, ops, opc, slot, cnt, fill, dinv = args
    _, rows, loads, blk = rhs.shape
    fills = fill.shape[2]
    own = rows * loads
    dims = (slabs, faces, rows, loads, blk, fills)
    small = (loads, rows, blk)
    hbm = pl.BlockSpec(memory_space=pltpu.HBM)
    dma = pltpu.SemaphoreType.DMA
    outs = pl.pallas_call(
        functools.partial(kernel, dims),
        out_shape=jax.ShapeDtypeStruct((2,) + small, F32),
        in_specs=[hbm] * 8,
        out_specs=pl.BlockSpec(memory_space=pltpu.VMEM),
        scratch_shapes=[
            pltpu.SMEM(slot.shape, jnp.int32),
            pltpu.SMEM(cnt.shape, jnp.int32),
            pltpu.VMEM(small, F32),
            pltpu.VMEM(small, F32),
            pltpu.VMEM(ops.shape[1:], F32),
            pltpu.VMEM(opc.shape[1:], F32),
            pltpu.VMEM(fill.shape[1:], F32),
            pltpu.VMEM(dinv.shape[1:], F32),
            pltpu.VMEM(small, F32),
            pltpu.VMEM(small, F32),
            pltpu.VMEM(small, F32),
            pltpu.VMEM(small, F32),
            pltpu.VMEM((rows, 5 * blk, 2 * blk), BF16),
            pltpu.VMEM((rows, fills * blk, 2 * blk), BF16),
            pltpu.VMEM((rows, blk, 2 * blk), BF16),
            pltpu.VMEM((rows, 8, blk), F32),
            pltpu.VMEM((own, blk), F32),
            pltpu.VMEM((faces * own + 8, blk), F32),
            pltpu.VMEM((faces * own + 8, blk), F32),
            pltpu.VMEM((own, blk), F32),
            pltpu.VMEM((8, blk), F32),
            pltpu.VMEM((8, blk), F32),
            dma((8,)),
            dma((4,)),
            dma((4,)),
            dma((faces,)),
            dma((faces,)),
            dma((faces,)),
            dma((faces,)),
            dma((3,)),
            dma((3,)),
        ],
        compiler_params=pltpu.CompilerParams(
            collective_id=0, has_side_effects=True, vmem_limit_bytes=60 * 2**20
        ),
        cost_estimate=pl.CostEstimate(
            flops=2 * rows * (2 * 5 + fills + 1) * blk * blk * loads,
            bytes_accessed=4 * rows * (6 + fills) * blk * blk,
            transcendentals=0,
        ),
    )(jnp.swapaxes(rhs, 1, 2), jnp.swapaxes(it, 1, 2), ops, opc, slot, cnt, fill, dinv)
    return tuple(jnp.swapaxes(outs[n : n + 1], 1, 2) for n in (0, 1))


def solution(mesh):
    four = P("slab", "face", None, None)
    five = P("slab", "face", None, None, None)
    return jax.shard_map(
        functools.partial(body, mesh.shape["slab"], mesh.shape["face"]),
        mesh=mesh,
        in_specs=(four, four, four, five, P("slab", "face", None), P("slab", "face"), five, four),
        out_specs=(four, four),
        check_vma=False,
    )
```

```python
import functools

import jax
import jax.numpy as jnp
from jax import lax
from jax.experimental import pallas as pl
from jax.experimental.pallas import tpu as pltpu
from jax.sharding import PartitionSpec as P

MESH = pl.DeviceIdType.MESH
F32, BF16 = jnp.float32, jnp.bfloat16


def halves(x):
    high = x.astype(BF16)
    return high, (x - high.astype(F32)).astype(BF16)


def rows_of(v):
    high = v.astype(BF16).astype(F32)
    return jnp.concatenate([high, v - high], axis=0).astype(BF16)


def product(x, w):
    y = jnp.dot(x, w, preferred_element_type=F32)
    n = w.shape[1] // 2
    return y[:8, :n] + (y[:8, n:] + y[8:, :n])


def kernel(
    dims,
    rhs, it, ops, opc, slot_in, cnt_in, fill, dinv,
    out,
    slot, cnt, v_rhs, v_it, v_ops, v_opc, v_fill, v_dinv,
    it_prev, it_next, it_lo, it_hi,
    w_op, w_fill, w_inv,
    part, sol, win1, win2, s_next, s_lo, s_hi,
    load_sem, it_send, it_recv, one_send, one_recv, two_send, two_recv, near_send, near_recv,
):
    slabs, faces, rows, loads, blk, fills = dims
    s, f = lax.axis_index("slab"), lax.axis_index("face")
    own = rows * loads
    slab_rows = faces * rows
    has_prev, has_next = s > 0, s < slabs - 1
    has_lo, has_hi = f > 0, f < faces - 1

    pairs = (
        (it.at[0], v_it), (rhs.at[0], v_rhs), (ops.at[0], v_ops), (opc.at[0], v_opc),
        (dinv.at[0], v_dinv), (fill.at[0], v_fill), (slot_in, slot), (cnt_in, cnt),
    )
    loading = [
        pltpu.make_async_copy(a, b, load_sem.at[n]) for n, (a, b) in enumerate(pairs)
    ]
    for c in loading:
        c.start()

    barrier = pltpu.get_barrier_semaphore()

    def greet(ok, who):
        @pl.when(ok)
        def _():
            pl.semaphore_signal(barrier, inc=1, device_id=who, device_id_type=MESH)

    greet(has_next, (s + 1, f))
    greet(has_lo, (s, f - 1))
    greet(has_hi, (s, f + 1))
    for g in range(faces):
        greet(has_prev, (s - 1, g))
    for g in range(faces):
        greet(s > 1, (s - 2, g))

    for c in loading[:4]:
        c.wait()

    for r in range(rows):
        blocks = (v_ops[r], v_opc[r, 0], v_opc[r, 2], v_opc[r, 3], v_opc[r, 1])
        for n, m in enumerate(blocks):
            high, low = halves(m.T)
            w_op[r, n * blk : (n + 1) * blk, :blk] = high
            w_op[r, n * blk : (n + 1) * blk, blk:] = low
    peers = has_prev.astype(jnp.int32) + has_lo.astype(jnp.int32) + has_hi.astype(jnp.int32)
    peers = peers + faces * (has_next.astype(jnp.int32) + (s < slabs - 2).astype(jnp.int32))
    pl.semaphore_wait(barrier, peers)

    def remote(src, dst, a, b, who):
        return pltpu.make_async_remote_copy(
            src_ref=src, dst_ref=dst, send_sem=a, recv_sem=b, device_id=who, device_id_type=MESH
        )

    halo = (
        (has_next, has_prev, v_it, it_prev, (s + 1, f)),
        (has_prev, has_next, v_it, it_next, (s - 1, f)),
        (has_hi, has_lo, v_it, it_lo, (s, f + 1)),
        (has_lo, has_hi, v_it, it_hi, (s, f - 1)),
    )
    halo_copies = []
    for n, (sends, gets, src, dst, who) in enumerate(halo):
        c = remote(src, dst, it_send.at[n], it_recv.at[n], who)
        halo_copies.append(c)
        pl.when(sends)(c.start)

        @pl.when(jnp.logical_not(gets))
        def _(dst=dst):
            dst[...] = jnp.zeros_like(dst)

    @pl.when(jnp.logical_not(has_prev))
    def _():
        win1[...] = jnp.zeros_like(win1)

    @pl.when(jnp.logical_not(has_next))
    def _():
        s_next[...] = jnp.zeros_like(s_next)

    @pl.when(jnp.logical_not(has_lo))
    def _():
        s_lo[...] = jnp.zeros_like(s_lo)

    @pl.when(jnp.logical_not(has_hi))
    def _():
        s_hi[...] = jnp.zeros_like(s_hi)

    loading[4].wait()
    for r in range(rows):
        high, low = halves(v_dinv[r].T)
        w_inv[r, :, :blk] = high
        w_inv[r, :, blk:] = low

    for c, (sends, gets, *_) in zip(halo_copies, halo):
        pl.when(gets)(c.wait_recv)

    fill_up = jnp.zeros((8 - loads, blk), F32)

    def up(v):
        return jnp.concatenate([v, fill_up], axis=0)

    for r in range(rows):
        before = it_lo[:, rows - 1] if r == 0 else v_it[:, r - 1]
        after = it_hi[:, 0] if r == rows - 1 else v_it[:, r + 1]
        x = jnp.concatenate(
            [rows_of(up(v)) for v in (v_it[:, r], it_prev[:, r], before, after, it_next[:, r])], axis=1
        )
        residual = up(v_rhs[:, r]) - product(x, w_op[r])
        part[r] = product(rows_of(residual), w_inv[r])

    def to_next(g):
        return remote(
            sol, win1.at[pl.ds(f * own, own)], one_send.at[g], one_recv.at[f], (s + 1, g)
        )

    def to_second(g):
        return remote(
            sol, win2.at[pl.ds(f * own, own)], two_send.at[g], two_recv.at[f], (s + 2, g)
        )

    def arrive(win, sem, g):
        return remote(sol, win.at[pl.ds(g * own, own)], one_send.at[g], sem.at[g], (s, f))

    near = (
        (has_prev, has_next, sol, s_next, (s - 1, f)),
        (has_hi, has_lo, sol.at[pl.ds(own - 8, 8)], s_lo, (s, f + 1)),
        (has_lo, has_hi, sol.at[pl.ds(0, 8)], s_hi, (s, f - 1)),
    )
    near_copies = [
        remote(src, dst, near_send.at[n], near_recv.at[n], who)
        for n, (_, _, src, dst, who) in enumerate(near)
    ]

    def spread():
        @pl.when(has_next)
        def _():
            for g in range(faces):
                to_next(g).start()

        for c, (sends, *_) in zip(near_copies[1:], near[1:]):
            pl.when(sends)(c.start)
        pl.when(has_prev)(near_copies[0].start)

        @pl.when(s < slabs - 2)
        def _():
            for g in range(faces):
                to_second(g).start()

    @pl.when(jnp.logical_not(has_prev))
    def _():
        for r in range(rows):
            sol[r * loads : (r + 1) * loads] = part[r][:loads]
        spread()

    for c in loading[5:]:
        c.wait()

    @pl.when(has_prev)
    def _():
        for r in range(rows):
            left = jnp.concatenate(halves(v_dinv[r]), axis=1)
            for k in range(fills):
                high, low = halves(v_fill[r, k])
                right = jnp.concatenate(
                    [
                        jnp.concatenate([high, low], axis=1),
                        jnp.concatenate([high, jnp.zeros_like(low)], axis=1),
                    ],
                    axis=0,
                )
                y = jnp.dot(left, right, preferred_element_type=F32)
                high, low = halves((y[:, :blk] + y[:, blk:]).T)
                w_fill[r, k * blk : (k + 1) * blk, :blk] = high
                w_fill[r, k * blk : (k + 1) * blk, blk:] = low

    def gathered(win, r, base):
        xs = []
        for k in range(fills):
            q = slot[0, r, k] - base
            ok = jnp.logical_and(jnp.logical_and(q >= 0, q < slab_rows), k < cnt[0, r])
            q = jnp.clip(q, 0, slab_rows - 1)
            v = win[pl.ds(q * loads, 8), :]
            xs.append(rows_of(jnp.where(ok, v, 0.0)))
        return jnp.concatenate(xs, axis=1)

    @pl.when(s > 1)
    def _():
        for g in range(faces):
            arrive(win2, two_recv, g).wait_recv()
        for r in range(rows):
            part[r] = part[r] - product(gathered(win2, r, 0), w_fill[r])

    @pl.when(has_prev)
    def _():
        for g in range(faces):
            arrive(win1, one_recv, g).wait_recv()
        for r in range(rows):
            y = part[r] - product(gathered(win1, r, slab_rows), w_fill[r])
            sol[r * loads : (r + 1) * loads] = y[:loads]
        spread()

    for r in range(rows):
        out[0, :, r] = sol[r * loads : (r + 1) * loads]

    def mine(ref, r):
        return rows_of(up(ref[r * loads : (r + 1) * loads]))

    for r in range(rows):
        x = jnp.concatenate(
            [
                mine(sol, r),
                rows_of(up(win1[pl.ds(f * own + r * loads, loads), :])),
            ],
            axis=1,
        )
        part[r] = product(x, w_op[r, : 2 * blk])
    for c, (_, gets, *_) in zip(near_copies[1:], near[1:]):
        pl.when(gets)(c.wait_recv)
    for r in range(rows):
        before = rows_of(up(s_lo[8 - loads :])) if r == 0 else mine(sol, r - 1)
        after = rows_of(up(s_hi[:loads])) if r == rows - 1 else mine(sol, r + 1)
        x = jnp.concatenate([before, after], axis=1)
        part[r] = part[r] + product(x, w_op[r, 2 * blk : 4 * blk])
    pl.when(has_next)(near_copies[0].wait_recv)
    for r in range(rows):
        y = part[r] + product(mine(s_next, r), w_op[r, 4 * blk :])
        out[1, :, r] = y[:loads]

    for c, (sends, *_) in zip(halo_copies, halo):
        pl.when(sends)(c.wait_send)
    for c, (sends, *_) in zip(near_copies, near):
        pl.when(sends)(c.wait_send)

    @pl.when(has_next)
    def _():
        for g in range(faces):
            to_next(g).wait_send()

    @pl.when(s < slabs - 2)
    def _():
        for g in range(faces):
            to_second(g).wait_send()


def body(slabs, faces, *args):
    rhs, it, ops, opc, slot, cnt, fill, dinv = args
    _, rows, loads, blk = rhs.shape
    fills = fill.shape[2]
    own = rows * loads
    dims = (slabs, faces, rows, loads, blk, fills)
    small = (loads, rows, blk)
    hbm = pl.BlockSpec(memory_space=pltpu.HBM)
    dma = pltpu.SemaphoreType.DMA
    outs = pl.pallas_call(
        functools.partial(kernel, dims),
        out_shape=pltpu.VMEM((2,) + small, F32),
        in_specs=[hbm] * 8,
        out_specs=pl.BlockSpec(memory_space=pltpu.VMEM),
        scratch_shapes=[
            pltpu.SMEM(slot.shape, jnp.int32),
            pltpu.SMEM(cnt.shape, jnp.int32),
            pltpu.VMEM(small, F32),
            pltpu.VMEM(small, F32),
            pltpu.VMEM(ops.shape[1:], F32),
            pltpu.VMEM(opc.shape[1:], F32),
            pltpu.VMEM(fill.shape[1:], F32),
            pltpu.VMEM(dinv.shape[1:], F32),
            pltpu.VMEM(small, F32),
            pltpu.VMEM(small, F32),
            pltpu.VMEM(small, F32),
            pltpu.VMEM(small, F32),
            pltpu.VMEM((rows, 5 * blk, 2 * blk), BF16),
            pltpu.VMEM((rows, fills * blk, 2 * blk), BF16),
            pltpu.VMEM((rows, blk, 2 * blk), BF16),
            pltpu.VMEM((rows, 8, blk), F32),
            pltpu.VMEM((own, blk), F32),
            pltpu.VMEM((faces * own + 8, blk), F32),
            pltpu.VMEM((faces * own + 8, blk), F32),
            pltpu.VMEM((own, blk), F32),
            pltpu.VMEM((8, blk), F32),
            pltpu.VMEM((8, blk), F32),
            dma((8,)),
            dma((4,)),
            dma((4,)),
            dma((faces,)),
            dma((faces,)),
            dma((faces,)),
            dma((faces,)),
            dma((3,)),
            dma((3,)),
        ],
        compiler_params=pltpu.CompilerParams(
            collective_id=0, has_side_effects=True, vmem_limit_bytes=60 * 2**20
        ),
        cost_estimate=pl.CostEstimate(
            flops=2 * rows * (2 * 5 + fills + 1) * blk * blk * loads,
            bytes_accessed=4 * rows * (6 + fills) * blk * blk,
            transcendentals=0,
        ),
    )(jnp.swapaxes(rhs, 1, 2), jnp.swapaxes(it, 1, 2), ops, opc, slot, cnt, fill, dinv)
    return tuple(jnp.swapaxes(outs[n : n + 1], 1, 2) for n in (0, 1))


def solution(mesh):
    four = P("slab", "face", None, None)
    five = P("slab", "face", None, None, None)
    return jax.shard_map(
        functools.partial(body, mesh.shape["slab"], mesh.shape["face"]),
        mesh=mesh,
        in_specs=(four, four, four, five, P("slab", "face", None), P("slab", "face"), five, four),
        out_specs=(four, four),
        check_vma=False,
    )
```

```python
import functools

import jax
import jax.numpy as jnp
from jax import lax
from jax.experimental import pallas as pl
from jax.experimental.pallas import tpu as pltpu
from jax.sharding import PartitionSpec as P

MESH = pl.DeviceIdType.MESH
F32, BF16 = jnp.float32, jnp.bfloat16


def halves(x):
    high = x.astype(BF16)
    return high, (x - high.astype(F32)).astype(BF16)


def rows_of(v):
    high = v.astype(BF16).astype(F32)
    return jnp.concatenate([high, v - high], axis=0).astype(BF16)


def product(x, w):
    y = jnp.dot(x, w, preferred_element_type=F32)
    n = w.shape[1] // 2
    return y[:8, :n] + (y[:8, n:] + y[8:, :n])


def kernel(
    dims,
    rhs, it, ops, opc, slot_in, cnt_in, fill, dinv,
    out,
    slot, cnt, v_rhs, v_it, v_ops, v_opc, v_fill, v_dinv,
    it_prev, it_next, it_lo, it_hi,
    w_op, w_fill, w_inv,
    part, sol, win1, win2, s_next, s_lo, s_hi,
    load_sem, it_send, it_recv, one_send, one_recv, two_send, two_recv, near_send, near_recv,
):
    slabs, faces, rows, loads, blk, fills = dims
    s, f = lax.axis_index("slab"), lax.axis_index("face")
    own = rows * loads
    slab_rows = faces * rows
    has_prev, has_next = s > 0, s < slabs - 1
    has_lo, has_hi = f > 0, f < faces - 1

    pairs = (
        (it.at[0], v_it), (rhs.at[0], v_rhs), (ops.at[0], v_ops), (opc.at[0], v_opc),
        (dinv.at[0], v_dinv), (fill.at[0], v_fill), (slot_in, slot), (cnt_in, cnt),
    )
    loading = [
        pltpu.make_async_copy(a, b, load_sem.at[n]) for n, (a, b) in enumerate(pairs)
    ]
    for c in loading:
        c.start()

    barrier = pltpu.get_barrier_semaphore()

    def greet(ok, who):
        @pl.when(ok)
        def _():
            pl.semaphore_signal(barrier, inc=1, device_id=who, device_id_type=MESH)

    greet(has_next, (s + 1, f))
    greet(has_lo, (s, f - 1))
    greet(has_hi, (s, f + 1))
    for g in range(faces):
        greet(has_prev, (s - 1, g))
    for g in range(faces):
        greet(s > 1, (s - 2, g))

    peers = has_prev.astype(jnp.int32) + has_lo.astype(jnp.int32) + has_hi.astype(jnp.int32)
    peers = peers + faces * (has_next.astype(jnp.int32) + (s < slabs - 2).astype(jnp.int32))
    pl.semaphore_wait(barrier, peers)

    def remote(src, dst, a, b, who):
        return pltpu.make_async_remote_copy(
            src_ref=src, dst_ref=dst, send_sem=a, recv_sem=b, device_id=who, device_id_type=MESH
        )

    loading[0].wait()

    halo = (
        (has_next, has_prev, v_it, it_prev, (s + 1, f)),
        (has_prev, has_next, v_it, it_next, (s - 1, f)),
        (has_hi, has_lo, v_it, it_lo, (s, f + 1)),
        (has_lo, has_hi, v_it, it_hi, (s, f - 1)),
    )
    halo_copies = []
    for n, (sends, gets, src, dst, who) in enumerate(halo):
        c = remote(src, dst, it_send.at[n], it_recv.at[n], who)
        halo_copies.append(c)
        pl.when(sends)(c.start)

        @pl.when(jnp.logical_not(gets))
        def _(dst=dst):
            dst[...] = jnp.zeros_like(dst)

    @pl.when(jnp.logical_not(has_prev))
    def _():
        win1[...] = jnp.zeros_like(win1)

    @pl.when(jnp.logical_not(has_next))
    def _():
        s_next[...] = jnp.zeros_like(s_next)

    @pl.when(jnp.logical_not(has_lo))
    def _():
        s_lo[...] = jnp.zeros_like(s_lo)

    @pl.when(jnp.logical_not(has_hi))
    def _():
        s_hi[...] = jnp.zeros_like(s_hi)

    for c in loading[1:4]:
        c.wait()

    for r in range(rows):
        blocks = (v_ops[r], v_opc[r, 0], v_opc[r, 2], v_opc[r, 3], v_opc[r, 1])
        for n, m in enumerate(blocks):
            high, low = halves(m.T)
            w_op[r, n * blk : (n + 1) * blk, :blk] = high
            w_op[r, n * blk : (n + 1) * blk, blk:] = low
    loading[4].wait()
    for r in range(rows):
        high, low = halves(v_dinv[r].T)
        w_inv[r, :, :blk] = high
        w_inv[r, :, blk:] = low

    for c, (sends, gets, *_) in zip(halo_copies, halo):
        pl.when(gets)(c.wait_recv)

    fill_up = jnp.zeros((8 - loads, blk), F32)

    def up(v):
        return jnp.concatenate([v, fill_up], axis=0)

    for r in range(rows):
        before = it_lo[:, rows - 1] if r == 0 else v_it[:, r - 1]
        after = it_hi[:, 0] if r == rows - 1 else v_it[:, r + 1]
        x = jnp.concatenate(
            [rows_of(up(v)) for v in (v_it[:, r], it_prev[:, r], before, after, it_next[:, r])], axis=1
        )
        residual = up(v_rhs[:, r]) - product(x, w_op[r])
        part[r] = product(rows_of(residual), w_inv[r])

    def to_next(g):
        return remote(
            sol, win1.at[pl.ds(f * own, own)], one_send.at[g], one_recv.at[f], (s + 1, g)
        )

    def to_second(g):
        return remote(
            sol, win2.at[pl.ds(f * own, own)], two_send.at[g], two_recv.at[f], (s + 2, g)
        )

    def arrive(win, sem, g):
        return remote(sol, win.at[pl.ds(g * own, own)], one_send.at[g], sem.at[g], (s, f))

    near = (
        (has_prev, has_next, sol, s_next, (s - 1, f)),
        (has_hi, has_lo, sol.at[pl.ds(own - 8, 8)], s_lo, (s, f + 1)),
        (has_lo, has_hi, sol.at[pl.ds(0, 8)], s_hi, (s, f - 1)),
    )
    near_copies = [
        remote(src, dst, near_send.at[n], near_recv.at[n], who)
        for n, (_, _, src, dst, who) in enumerate(near)
    ]

    def spread():
        @pl.when(has_next)
        def _():
            for g in range(faces):
                to_next(g).start()

        for c, (sends, *_) in zip(near_copies[1:], near[1:]):
            pl.when(sends)(c.start)
        pl.when(has_prev)(near_copies[0].start)

        @pl.when(s < slabs - 2)
        def _():
            for g in range(faces):
                to_second(g).start()

    @pl.when(jnp.logical_not(has_prev))
    def _():
        for r in range(rows):
            sol[r * loads : (r + 1) * loads] = part[r][:loads]
        spread()

    for c in loading[5:]:
        c.wait()

    @pl.when(has_prev)
    def _():
        for r in range(rows):
            left = jnp.concatenate(halves(v_dinv[r]), axis=1)
            for k in range(fills):
                high, low = halves(v_fill[r, k])
                right = jnp.concatenate(
                    [
                        jnp.concatenate([high, low], axis=1),
                        jnp.concatenate([high, jnp.zeros_like(low)], axis=1),
                    ],
                    axis=0,
                )
                y = jnp.dot(left, right, preferred_element_type=F32)
                high, low = halves((y[:, :blk] + y[:, blk:]).T)
                w_fill[r, k * blk : (k + 1) * blk, :blk] = high
                w_fill[r, k * blk : (k + 1) * blk, blk:] = low

    def gathered(win, r, base):
        xs = []
        for k in range(fills):
            q = slot[0, r, k] - base
            ok = jnp.logical_and(jnp.logical_and(q >= 0, q < slab_rows), k < cnt[0, r])
            q = jnp.clip(q, 0, slab_rows - 1)
            v = win[pl.ds(q * loads, 8), :]
            xs.append(rows_of(jnp.where(ok, v, 0.0)))
        return jnp.concatenate(xs, axis=1)

    @pl.when(s > 1)
    def _():
        for g in range(faces):
            arrive(win2, two_recv, g).wait_recv()
        for r in range(rows):
            part[r] = part[r] - product(gathered(win2, r, 0), w_fill[r])

    @pl.when(has_prev)
    def _():
        for g in range(faces):
            arrive(win1, one_recv, g).wait_recv()
        for r in range(rows):
            y = part[r] - product(gathered(win1, r, slab_rows), w_fill[r])
            sol[r * loads : (r + 1) * loads] = y[:loads]
        spread()

    for r in range(rows):
        out[0, :, r] = sol[r * loads : (r + 1) * loads]

    def mine(ref, r):
        return rows_of(up(ref[r * loads : (r + 1) * loads]))

    def beside(r, n):
        return w_op[r, n * blk : (n + 1) * blk]

    for r in range(rows):
        earlier = rows_of(up(win1[pl.ds(f * own + r * loads, loads), :]))
        y = product(jnp.concatenate([mine(sol, r), earlier], axis=1), w_op[r, : 2 * blk])
        if r > 0:
            y = y + product(mine(sol, r - 1), beside(r, 2))
        if r < rows - 1:
            y = y + product(mine(sol, r + 1), beside(r, 3))
        part[r] = y
    for c, (_, gets, *_) in zip(near_copies[1:], near[1:]):
        pl.when(gets)(c.wait_recv)
    part[0] = part[0] + product(rows_of(up(s_lo[8 - loads :])), beside(0, 2))
    last = rows - 1
    part[last] = part[last] + product(rows_of(up(s_hi[:loads])), beside(last, 3))
    pl.when(has_next)(near_copies[0].wait_recv)
    for r in range(rows):
        y = part[r] + product(mine(s_next, r), w_op[r, 4 * blk :])
        out[1, :, r] = y[:loads]

    for c, (sends, *_) in zip(halo_copies, halo):
        pl.when(sends)(c.wait_send)
    for c, (sends, *_) in zip(near_copies, near):
        pl.when(sends)(c.wait_send)

    @pl.when(has_next)
    def _():
        for g in range(faces):
            to_next(g).wait_send()

    @pl.when(s < slabs - 2)
    def _():
        for g in range(faces):
            to_second(g).wait_send()


def body(slabs, faces, *args):
    rhs, it, ops, opc, slot, cnt, fill, dinv = args
    _, rows, loads, blk = rhs.shape
    fills = fill.shape[2]
    own = rows * loads
    dims = (slabs, faces, rows, loads, blk, fills)
    small = (loads, rows, blk)
    hbm = pl.BlockSpec(memory_space=pltpu.HBM)
    dma = pltpu.SemaphoreType.DMA
    outs = pl.pallas_call(
        functools.partial(kernel, dims),
        out_shape=pltpu.VMEM((2,) + small, F32),
        in_specs=[hbm] * 8,
        out_specs=pl.BlockSpec(memory_space=pltpu.VMEM),
        scratch_shapes=[
            pltpu.SMEM(slot.shape, jnp.int32),
            pltpu.SMEM(cnt.shape, jnp.int32),
            pltpu.VMEM(small, F32),
            pltpu.VMEM(small, F32),
            pltpu.VMEM(ops.shape[1:], F32),
            pltpu.VMEM(opc.shape[1:], F32),
            pltpu.VMEM(fill.shape[1:], F32),
            pltpu.VMEM(dinv.shape[1:], F32),
            pltpu.VMEM(small, F32),
            pltpu.VMEM(small, F32),
            pltpu.VMEM(small, F32),
            pltpu.VMEM(small, F32),
            pltpu.VMEM((rows, 5 * blk, 2 * blk), BF16),
            pltpu.VMEM((rows, fills * blk, 2 * blk), BF16),
            pltpu.VMEM((rows, blk, 2 * blk), BF16),
            pltpu.VMEM((rows, 8, blk), F32),
            pltpu.VMEM((own, blk), F32),
            pltpu.VMEM((faces * own + 8, blk), F32),
            pltpu.VMEM((faces * own + 8, blk), F32),
            pltpu.VMEM((own, blk), F32),
            pltpu.VMEM((8, blk), F32),
            pltpu.VMEM((8, blk), F32),
            dma((8,)),
            dma((4,)),
            dma((4,)),
            dma((faces,)),
            dma((faces,)),
            dma((faces,)),
            dma((faces,)),
            dma((3,)),
            dma((3,)),
        ],
        compiler_params=pltpu.CompilerParams(
            collective_id=0, has_side_effects=True, vmem_limit_bytes=60 * 2**20
        ),
        cost_estimate=pl.CostEstimate(
            flops=2 * rows * (2 * 5 + fills + 1) * blk * blk * loads,
            bytes_accessed=4 * rows * (6 + fills) * blk * blk,
            transcendentals=0,
        ),
    )(jnp.swapaxes(rhs, 1, 2), jnp.swapaxes(it, 1, 2), ops, opc, slot, cnt, fill, dinv)
    return tuple(jnp.swapaxes(outs[n : n + 1], 1, 2) for n in (0, 1))


def solution(mesh):
    four = P("slab", "face", None, None)
    five = P("slab", "face", None, None, None)
    return jax.shard_map(
        functools.partial(body, mesh.shape["slab"], mesh.shape["face"]),
        mesh=mesh,
        in_specs=(four, four, four, five, P("slab", "face", None), P("slab", "face"), five, four),
        out_specs=(four, four),
        check_vma=False,
    )
```

```python
import functools

import jax
import jax.numpy as jnp
from jax import lax
from jax.experimental import pallas as pl
from jax.experimental.pallas import tpu as pltpu
from jax.sharding import PartitionSpec as P

MESH = pl.DeviceIdType.MESH
F32, BF16 = jnp.float32, jnp.bfloat16


def halves(x):
    high = x.astype(BF16)
    return high, (x - high.astype(F32)).astype(BF16)


def rows_of(v):
    high = v.astype(BF16).astype(F32)
    return jnp.concatenate([high, v - high], axis=0).astype(BF16)


def product(x, w):
    y = jnp.dot(x, w, preferred_element_type=F32)
    n = w.shape[1] // 2
    return y[:8, :n] + (y[:8, n:] + y[8:, :n])


def kernel(
    dims,
    rhs, it, ops, opc, slot_in, cnt_in, fill, dinv,
    out,
    slot, cnt, v_rhs, v_it, v_ops, v_opc, v_fill, v_dinv,
    it_prev, it_next, it_lo, it_hi,
    w_op, w_fill, w_inv,
    part, sol, win1, win2, s_next, s_lo, s_hi,
    load_sem, it_send, it_recv, one_send, one_recv, two_send, two_recv, near_send, near_recv,
):
    slabs, faces, rows, loads, blk, fills = dims
    s, f = lax.axis_index("slab"), lax.axis_index("face")
    own = rows * loads
    slab_rows = faces * rows
    has_prev, has_next = s > 0, s < slabs - 1
    has_lo, has_hi = f > 0, f < faces - 1

    pairs = (
        (it.at[0], v_it), (rhs.at[0], v_rhs), (ops.at[0], v_ops), (opc.at[0], v_opc),
        (dinv.at[0], v_dinv), (fill.at[0], v_fill), (slot_in, slot), (cnt_in, cnt),
    )
    loading = [
        pltpu.make_async_copy(a, b, load_sem.at[n]) for n, (a, b) in enumerate(pairs)
    ]
    for c in loading:
        c.start()

    barrier = pltpu.get_barrier_semaphore()

    def greet(ok, who):
        @pl.when(ok)
        def _():
            pl.semaphore_signal(barrier, inc=1, device_id=who, device_id_type=MESH)

    greet(has_next, (s + 1, f))
    greet(has_lo, (s, f - 1))
    greet(has_hi, (s, f + 1))
    for g in range(faces):
        greet(has_prev, (s - 1, g))
    for g in range(faces):
        greet(s > 1, (s - 2, g))

    peers = has_prev.astype(jnp.int32) + has_lo.astype(jnp.int32) + has_hi.astype(jnp.int32)
    peers = peers + faces * (has_next.astype(jnp.int32) + (s < slabs - 2).astype(jnp.int32))
    pl.semaphore_wait(barrier, peers)

    def remote(src, dst, a, b, who):
        return pltpu.make_async_remote_copy(
            src_ref=src, dst_ref=dst, send_sem=a, recv_sem=b, device_id=who, device_id_type=MESH
        )

    loading[0].wait()

    halo = (
        (has_next, has_prev, v_it, it_prev, (s + 1, f)),
        (has_prev, has_next, v_it, it_next, (s - 1, f)),
        (has_hi, has_lo, v_it, it_lo, (s, f + 1)),
        (has_lo, has_hi, v_it, it_hi, (s, f - 1)),
    )
    halo_copies = []
    for n, (sends, gets, src, dst, who) in enumerate(halo):
        c = remote(src, dst, it_send.at[n], it_recv.at[n], who)
        halo_copies.append(c)
        pl.when(sends)(c.start)

        @pl.when(jnp.logical_not(gets))
        def _(dst=dst):
            dst[...] = jnp.zeros_like(dst)

    @pl.when(jnp.logical_not(has_prev))
    def _():
        win1[...] = jnp.zeros_like(win1)

    @pl.when(jnp.logical_not(has_next))
    def _():
        s_next[...] = jnp.zeros_like(s_next)

    @pl.when(jnp.logical_not(has_lo))
    def _():
        s_lo[...] = jnp.zeros_like(s_lo)

    @pl.when(jnp.logical_not(has_hi))
    def _():
        s_hi[...] = jnp.zeros_like(s_hi)

    for c in loading[1:4]:
        c.wait()

    for r in range(rows):
        blocks = (v_ops[r], v_opc[r, 0], v_opc[r, 2], v_opc[r, 3], v_opc[r, 1])
        for n, m in enumerate(blocks):
            high, low = halves(m.T)
            w_op[r, n * blk : (n + 1) * blk, :blk] = high
            w_op[r, n * blk : (n + 1) * blk, blk:] = low
    loading[4].wait()
    for r in range(rows):
        high, low = halves(v_dinv[r].T)
        w_inv[r, :, :blk] = high
        w_inv[r, :, blk:] = low

    for c, (sends, gets, *_) in zip(halo_copies, halo):
        pl.when(gets)(c.wait_recv)

    fill_up = jnp.zeros((8 - loads, blk), F32)

    def up(v):
        return jnp.concatenate([v, fill_up], axis=0)

    for r in range(rows):
        before = it_lo[:, rows - 1] if r == 0 else v_it[:, r - 1]
        after = it_hi[:, 0] if r == rows - 1 else v_it[:, r + 1]
        x = jnp.concatenate(
            [rows_of(up(v)) for v in (v_it[:, r], it_prev[:, r], before, after, it_next[:, r])], axis=1
        )
        residual = up(v_rhs[:, r]) - product(x, w_op[r])
        part[r] = product(rows_of(residual), w_inv[r])

    def target(n):
        return lax.rem(f + faces // 2 + n, faces)

    def to_next(n):
        return remote(
            sol, win1.at[pl.ds(f * own, own)], one_send.at[n], one_recv.at[f], (s + 1, target(n))
        )

    def to_second(n):
        return remote(
            sol, win2.at[pl.ds(f * own, own)], two_send.at[n], two_recv.at[f], (s + 2, target(n))
        )

    def arrive(win, sem, g):
        return remote(sol, win.at[pl.ds(g * own, own)], one_send.at[g], sem.at[g], (s, f))

    near = (
        (has_prev, has_next, sol, s_next, (s - 1, f)),
        (has_hi, has_lo, sol.at[pl.ds(own - 8, 8)], s_lo, (s, f + 1)),
        (has_lo, has_hi, sol.at[pl.ds(0, 8)], s_hi, (s, f - 1)),
    )
    near_copies = [
        remote(src, dst, near_send.at[n], near_recv.at[n], who)
        for n, (_, _, src, dst, who) in enumerate(near)
    ]

    def spread():
        @pl.when(has_next)
        def _():
            for g in range(faces):
                to_next(g).start()

        for c, (sends, *_) in zip(near_copies[1:], near[1:]):
            pl.when(sends)(c.start)
        pl.when(has_prev)(near_copies[0].start)

        @pl.when(s < slabs - 2)
        def _():
            for g in range(faces):
                to_second(g).start()

    @pl.when(jnp.logical_not(has_prev))
    def _():
        for r in range(rows):
            sol[r * loads : (r + 1) * loads] = part[r][:loads]
        spread()

    for c in loading[5:]:
        c.wait()

    @pl.when(has_prev)
    def _():
        for r in range(rows):
            left = jnp.concatenate(halves(v_dinv[r]), axis=1)
            for k in range(fills):
                high, low = halves(v_fill[r, k])
                right = jnp.concatenate(
                    [
                        jnp.concatenate([high, low], axis=1),
                        jnp.concatenate([high, jnp.zeros_like(low)], axis=1),
                    ],
                    axis=0,
                )
                y = jnp.dot(left, right, preferred_element_type=F32)
                high, low = halves((y[:, :blk] + y[:, blk:]).T)
                w_fill[r, k * blk : (k + 1) * blk, :blk] = high
                w_fill[r, k * blk : (k + 1) * blk, blk:] = low

    def gathered(win, r, base):
        xs = []
        for k in range(fills):
            q = slot[0, r, k] - base
            ok = jnp.logical_and(jnp.logical_and(q >= 0, q < slab_rows), k < cnt[0, r])
            q = jnp.clip(q, 0, slab_rows - 1)
            v = win[pl.ds(q * loads, 8), :]
            xs.append(rows_of(jnp.where(ok, v, 0.0)))
        return jnp.concatenate(xs, axis=1)

    @pl.when(s > 1)
    def _():
        for g in range(faces):
            arrive(win2, two_recv, g).wait_recv()
        for r in range(rows):
            part[r] = part[r] - product(gathered(win2, r, 0), w_fill[r])

    @pl.when(has_prev)
    def _():
        for g in range(faces):
            arrive(win1, one_recv, g).wait_recv()
        for r in range(rows):
            y = part[r] - product(gathered(win1, r, slab_rows), w_fill[r])
            sol[r * loads : (r + 1) * loads] = y[:loads]
        spread()

    for r in range(rows):
        out[0, :, r] = sol[r * loads : (r + 1) * loads]

    def mine(ref, r):
        return rows_of(up(ref[r * loads : (r + 1) * loads]))

    def beside(r, n):
        return w_op[r, n * blk : (n + 1) * blk]

    for r in range(rows):
        earlier = rows_of(up(win1[pl.ds(f * own + r * loads, loads), :]))
        y = product(jnp.concatenate([mine(sol, r), earlier], axis=1), w_op[r, : 2 * blk])
        if r > 0:
            y = y + product(mine(sol, r - 1), beside(r, 2))
        if r < rows - 1:
            y = y + product(mine(sol, r + 1), beside(r, 3))
        part[r] = y
    for c, (_, gets, *_) in zip(near_copies[1:], near[1:]):
        pl.when(gets)(c.wait_recv)
    part[0] = part[0] + product(rows_of(up(s_lo[8 - loads :])), beside(0, 2))
    last = rows - 1
    part[last] = part[last] + product(rows_of(up(s_hi[:loads])), beside(last, 3))
    pl.when(has_next)(near_copies[0].wait_recv)
    for r in range(rows):
        y = part[r] + product(mine(s_next, r), w_op[r, 4 * blk :])
        out[1, :, r] = y[:loads]

    for c, (sends, *_) in zip(halo_copies, halo):
        pl.when(sends)(c.wait_send)
    for c, (sends, *_) in zip(near_copies, near):
        pl.when(sends)(c.wait_send)

    @pl.when(has_next)
    def _():
        for g in range(faces):
            to_next(g).wait_send()

    @pl.when(s < slabs - 2)
    def _():
        for g in range(faces):
            to_second(g).wait_send()


def body(slabs, faces, *args):
    rhs, it, ops, opc, slot, cnt, fill, dinv = args
    _, rows, loads, blk = rhs.shape
    fills = fill.shape[2]
    own = rows * loads
    dims = (slabs, faces, rows, loads, blk, fills)
    small = (loads, rows, blk)
    hbm = pl.BlockSpec(memory_space=pltpu.HBM)
    dma = pltpu.SemaphoreType.DMA
    outs = pl.pallas_call(
        functools.partial(kernel, dims),
        out_shape=pltpu.VMEM((2,) + small, F32),
        in_specs=[hbm] * 8,
        out_specs=pl.BlockSpec(memory_space=pltpu.VMEM),
        scratch_shapes=[
            pltpu.SMEM(slot.shape, jnp.int32),
            pltpu.SMEM(cnt.shape, jnp.int32),
            pltpu.VMEM(small, F32),
            pltpu.VMEM(small, F32),
            pltpu.VMEM(ops.shape[1:], F32),
            pltpu.VMEM(opc.shape[1:], F32),
            pltpu.VMEM(fill.shape[1:], F32),
            pltpu.VMEM(dinv.shape[1:], F32),
            pltpu.VMEM(small, F32),
            pltpu.VMEM(small, F32),
            pltpu.VMEM(small, F32),
            pltpu.VMEM(small, F32),
            pltpu.VMEM((rows, 5 * blk, 2 * blk), BF16),
            pltpu.VMEM((rows, fills * blk, 2 * blk), BF16),
            pltpu.VMEM((rows, blk, 2 * blk), BF16),
            pltpu.VMEM((rows, 8, blk), F32),
            pltpu.VMEM((own, blk), F32),
            pltpu.VMEM((faces * own + 8, blk), F32),
            pltpu.VMEM((faces * own + 8, blk), F32),
            pltpu.VMEM((own, blk), F32),
            pltpu.VMEM((8, blk), F32),
            pltpu.VMEM((8, blk), F32),
            dma((8,)),
            dma((4,)),
            dma((4,)),
            dma((faces,)),
            dma((faces,)),
            dma((faces,)),
            dma((faces,)),
            dma((3,)),
            dma((3,)),
        ],
        compiler_params=pltpu.CompilerParams(
            collective_id=0, has_side_effects=True, vmem_limit_bytes=60 * 2**20
        ),
        cost_estimate=pl.CostEstimate(
            flops=2 * rows * (2 * 5 + fills + 1) * blk * blk * loads,
            bytes_accessed=4 * rows * (6 + fills) * blk * blk,
            transcendentals=0,
        ),
    )(jnp.swapaxes(rhs, 1, 2), jnp.swapaxes(it, 1, 2), ops, opc, slot, cnt, fill, dinv)
    return tuple(jnp.swapaxes(outs[n : n + 1], 1, 2) for n in (0, 1))


def solution(mesh):
    four = P("slab", "face", None, None)
    five = P("slab", "face", None, None, None)
    return jax.shard_map(
        functools.partial(body, mesh.shape["slab"], mesh.shape["face"]),
        mesh=mesh,
        in_specs=(four, four, four, five, P("slab", "face", None), P("slab", "face"), five, four),
        out_specs=(four, four),
        check_vma=False,
    )
```
